32 devices in a mesh: groups: 2 (over y), panels: 8 (over z, core), rhs: 2 (over x).
Axes of the slice: x: 2, y: 2, z: 4, core: 2. Of those that a mesh axis runs over, the one named last changes fastest.
Arguments:
- incident: bfloat16 [32, 65536], P('rhs', ('groups', 'panels')), parts along dimension 1, may hold values from -16 to 16
- tree_order: int32 [65536], P(('groups', 'panels')), parts along dimension 0, may hold values from 0 to 32767, as said below
- near_rows: int32 [3072], P(('groups', 'panels', 'rhs')), parts along dimension 0, may hold values from 0 to 32, as said below
- near_sources: int32 [3072], P(('groups', 'panels', 'rhs')), parts along dimension 0, may hold values from 0 to 255, as said below
- near_blocks: bfloat16 [3072, 128, 128], P(('groups', 'panels', 'rhs')), parts along dimension 0, may hold values from -0.21875 to 0.21875
- far_rows: int32 [1472], P(('groups', 'panels', 'rhs')), parts along dimension 0, may hold values from 0 to 32, as said below
- far_sources: int32 [1472], P(('groups', 'panels', 'rhs')), parts along dimension 0, may hold values from 0 to 255, as said below
- far_left: bfloat16 [1472, 16, 128], P(('groups', 'panels', 'rhs')), parts along dimension 0, may hold values from -0.875 to 0.875
- far_right: bfloat16 [1472, 16, 128], P(('groups', 'panels', 'rhs')), parts along dimension 0, may hold values from -0.5 to 0.5
Outputs:
- first_image: float32 [32, 65536], P('rhs', ('groups', 'panels')), parts along dimension 1
- second_image: float32 [32, 65536], P('rhs', ('groups', 'panels')), parts along dimension 1
The draws below stay inside these ranges and needn't reach their ends.
There are 2 independent parts, one for each index of `groups`. The reference program is written for one: setup_inputs(seed, part) draws one part's arguments, and reference() takes and returns one part's arrays. A program takes and returns all parts, laid end to end along the dimension named above; each array names one. Nothing has to cross between parts.
Inputs may be any that keep to these rules, and one draw needn't show every extreme that they name: `tree_order`: tree positions of one owner's range of 4096 panels name panels of that same range, each once. `near_rows`: 32 marks padding; padding stands at the end of each device's list of 96 entries, and some device's list has none. `near_sources`: A live entry's source cluster lies within 2 clusters of its row cluster in global order; every entry's source lies within 2 clusters of its owner's range. `far_rows`: 32 marks padding; padding stands at the end of each device's list of 46 entries, and some device's list has none. `far_sources`: each device's far list names exactly 2 source clusters of every other owner and 32 of its own owner, in any order.
All inputs are finite; a program needn't handle non-finite values.
Results may differ from the reference program's by a relative error of at most 0.0041.
Values may be sent and summed in bfloat16 or wider, within the bound.
A program may use at most 64 MiB of HBM per device.

```python
import jax
import jax.numpy as jnp
from jax import lax

BLK = 128
RANK = 16
RHS = 32
CL_DEV = 32
NB_DEV = 96
NEAR_REACH = 2
FAR_PEER = 2
FAR_LOCAL = 32
PAN_DEV = 4096
CLUSTERS = 256
PANELS = 32768
FB_DEV = 46
NEAR_ALL = 1536
FAR_ALL = 736
N_PANELS = 8
N_RHS = 2


def near_layout(key):
    owners = CLUSTERS // CL_DEV
    devices = NEAR_ALL // NB_DEV
    shares = devices // owners
    keys = jax.random.split(key, 5)
    entry = jnp.arange(NB_DEV, dtype=jnp.int32)[None, :]
    device = jnp.arange(devices, dtype=jnp.int32)[:, None]
    owner = device // shares
    rows = jax.random.randint(keys[0], (devices, NB_DEV), 0, CL_DEV, dtype=jnp.int32)
    offsets = jax.random.randint(keys[1], (devices, NB_DEV), -NEAR_REACH, NEAR_REACH + 1, dtype=jnp.int32)
    outward = jax.random.randint(keys[2], (devices, NB_DEV), 1, NEAR_REACH + 1, dtype=jnp.int32)
    edge = entry < 4
    lower = entry % 2 == 0
    rows = jnp.where(edge, jnp.where(lower, 0, CL_DEV - 1), rows)
    offsets = jnp.where(edge, jnp.where(lower, -outward, outward), offsets)
    sources = jnp.clip(owner * CL_DEV + rows + offsets, 0, CLUSTERS - 1)
    live = jax.random.randint(keys[3], (devices, 1), NB_DEV // 2, NB_DEV + 1, dtype=jnp.int32)
    fullest = jax.random.randint(keys[4], (), 0, devices, dtype=jnp.int32)
    live = jnp.where(device == fullest, NB_DEV, live)
    rows = jnp.where(entry < live, rows, CL_DEV)
    return (rows.reshape(-1), sources.reshape(-1).astype(jnp.int32))


def far_layout(key):
    owners = CLUSTERS // CL_DEV
    devices = FAR_ALL // FB_DEV
    shares = devices // owners
    keys = jax.random.split(key, 5)
    entry = jnp.arange(FB_DEV, dtype=jnp.int32)
    device = jnp.arange(devices, dtype=jnp.int32)[:, None]
    owner = device // shares
    offset = jnp.where(entry < FAR_LOCAL, 0, (entry - FAR_LOCAL) // FAR_PEER + 1)
    orders = jax.vmap(lambda k: jax.random.permutation(k, FB_DEV))(jax.random.split(keys[0], devices))
    shuffled = offset[orders.astype(jnp.int32)]
    target = (owner + shuffled) % owners
    within = jax.random.randint(keys[1], (devices, FB_DEV), 0, CL_DEV, dtype=jnp.int32)
    sources = target * CL_DEV + within
    rows = jax.random.randint(keys[2], (devices, FB_DEV), 0, CL_DEV, dtype=jnp.int32)
    live = jax.random.randint(keys[3], (devices, 1), FB_DEV // 2, FB_DEV + 1, dtype=jnp.int32)
    fullest = jax.random.randint(keys[4], (), 0, devices, dtype=jnp.int32)
    live = jnp.where(device == fullest, FB_DEV, live)
    rows = jnp.where(entry[None, :] < live, rows, CL_DEV)
    return (rows.reshape(-1), sources.reshape(-1).astype(jnp.int32))


def draw_near_rows(key, part):
    return near_layout(key)[0]


def draw_near_sources(key, part):
    return near_layout(key)[1]


def draw_far_rows(key, part):
    return far_layout(jax.random.fold_in(key, 5))[0]


def draw_far_sources(key, part):
    return far_layout(jax.random.fold_in(key, 5))[1]


def draw_tree_order(key, part):
    key = jax.random.fold_in(key, 7)
    owners = PANELS // PAN_DEV
    orders = jax.vmap(lambda k: jax.random.permutation(k, PAN_DEV))(jax.random.split(key, owners))
    starts = jnp.arange(owners, dtype=jnp.int32)[:, None] * PAN_DEV
    return (orders.astype(jnp.int32) + starts).reshape(-1)


def draw_incident(key, part):
    key = jax.random.fold_in(key, 11)
    position = jnp.arange(PANELS, dtype=jnp.float32) / PANELS
    amplitude = 1.0 + 3.0 * position
    values = jnp.clip(jax.random.normal(key, (RHS, PANELS), jnp.float32), -4.0, 4.0)
    return (values * amplitude[None, :]).astype(jnp.bfloat16)


def shard_levels(key, dims, cuts, least, largest):
    def one(dim, blocks):
        draws = jax.random.uniform(jax.random.fold_in(jax.random.fold_in(key, 6), dim), (blocks,), jnp.float32, least / len(cuts), largest / len(cuts))
        return jnp.repeat(jnp.exp(draws), dims[dim] // blocks).reshape((-1,) + (1,) * (len(dims) - dim - 1))

    factor_of = one(*cuts[0])
    for cut in cuts[1:]:
        factor_of = factor_of * one(*cut)
    return factor_of


def centred(key, shape, deviation, reach, shards=(), held_as=jnp.bfloat16):
    array = deviation * jax.random.normal(key, shape, jnp.float32)
    if shards:
        array = array * shard_levels(key, shape, shards, -0.22, 0.18)
    return jnp.clip(array, -reach, reach).astype(held_as)


def setup_inputs(seed: int = 0, part: int = 0) -> dict:
    key_of = jax.random.split(jax.random.key(seed), 10)
    part_splits = jax.random.split(jax.random.fold_in(key_of[9], part), 10)
    incident = draw_incident(jax.random.fold_in(jax.random.fold_in(key_of[9], part), 71), part)
    tree_order = draw_tree_order(jax.random.fold_in(jax.random.fold_in(key_of[9], part), 71), part)
    near_rows = draw_near_rows(jax.random.fold_in(jax.random.fold_in(key_of[9], part), 71), part)
    near_sources = draw_near_sources(jax.random.fold_in(jax.random.fold_in(key_of[9], part), 71), part)
    near_blocks = centred(part_splits[4], (NEAR_ALL, BLK, BLK), (BLK * NB_DEV * N_RHS // CL_DEV) ** -0.5, 0.21875, ((0, 16),))
    far_rows = draw_far_rows(jax.random.fold_in(jax.random.fold_in(key_of[9], part), 71), part)
    far_sources = draw_far_sources(jax.random.fold_in(jax.random.fold_in(key_of[9], part), 71), part)
    far_left = centred(part_splits[7], (FAR_ALL, RANK, BLK), (RANK * FB_DEV * N_RHS // CL_DEV) ** -0.5, 0.875, ((0, 16),))
    far_right = centred(part_splits[8], (FAR_ALL, RANK, BLK), BLK ** -0.5, 0.5, ((0, 16),))
    return {"incident": incident, "tree_order": tree_order, "near_rows": near_rows, "near_sources": near_sources, "near_blocks": near_blocks, "far_rows": far_rows, "far_sources": far_sources, "far_left": far_left, "far_right": far_right}


def operate(field, near_rows, near_sources, near_blocks, far_rows, far_sources, far_left, far_right):
    segments = field.reshape(RHS, CLUSTERS, BLK)
    near_span = NB_DEV * N_RHS
    far_span = FB_DEV * N_RHS
    cluster_ids = jnp.arange(CL_DEV, dtype=jnp.int32)
    highest = lax.Precision.HIGHEST

    def one_owner(owner):
        near_start = owner * near_span
        far_start = owner * far_span
        rows = lax.dynamic_slice_in_dim(near_rows, near_start, near_span, 0)
        sources = lax.dynamic_slice_in_dim(near_sources, near_start, near_span, 0)
        blocks = lax.dynamic_slice_in_dim(near_blocks, near_start, near_span, 0).astype(jnp.float32)
        near_input = segments[:, sources].astype(jnp.float32)
        near_terms = jnp.einsum('ekj,hej->hek', blocks, near_input, precision=highest)
        near_hot = (rows[:, None] == cluster_ids[None, :]).astype(jnp.float32)
        placed = jnp.einsum('ec,hek->hck', near_hot, near_terms, precision=highest)
        frows = lax.dynamic_slice_in_dim(far_rows, far_start, far_span, 0)
        fsources = lax.dynamic_slice_in_dim(far_sources, far_start, far_span, 0)
        lefts = lax.dynamic_slice_in_dim(far_left, far_start, far_span, 0).astype(jnp.float32)
        rights = lax.dynamic_slice_in_dim(far_right, far_start, far_span, 0).astype(jnp.float32)
        far_input = segments[:, fsources].astype(jnp.float32)
        coefficients = jnp.einsum('emj,hej->hem', rights, far_input, precision=highest).astype(jnp.bfloat16)
        coefficients = lax.optimization_barrier(coefficients).astype(jnp.float32)
        far_terms = jnp.einsum('emk,hem->hek', lefts, coefficients, precision=highest)
        far_hot = (frows[:, None] == cluster_ids[None, :]).astype(jnp.float32)
        placed = placed + jnp.einsum('ec,hek->hck', far_hot, far_terms, precision=highest)
        return placed
    stacked = lax.map(one_owner, jnp.arange(N_PANELS, dtype=jnp.int32))
    return jnp.transpose(stacked, (1, 0, 2, 3)).reshape(RHS, PANELS)

def reference(incident, tree_order, near_rows, near_sources, near_blocks, far_rows, far_sources, far_left, far_right):
    lists = (near_rows, near_sources, near_blocks, far_rows, far_sources, far_left, far_right)
    tree = incident[:, tree_order]
    first_tree = operate(tree, *lists)
    squares = lax.optimization_barrier(jnp.sum(first_tree * first_tree, axis=1))
    scale = lax.rsqrt(squares / PANELS + 1e-06)
    normed = (first_tree * scale[:, None]).astype(jnp.bfloat16)
    second_tree = operate(normed, *lists)
    first_image = jnp.zeros((RHS, PANELS), jnp.float32).at[:, tree_order].set(first_tree)
    second_image = jnp.zeros((RHS, PANELS), jnp.float32).at[:, tree_order].set(second_tree)
    return (first_image, second_image)
```

```python
import functools

import jax
import jax.numpy as jnp
from jax import lax
from jax.experimental import pallas as pl
from jax.experimental.pallas import tpu as pltpu
from jax.sharding import PartitionSpec as P

MESH = pl.DeviceIdType.MESH
REACH = 2
CAPACITY = 2
LAST = (((1,), (1,)), ((), ()))
CHUNKS = 4
ROWS = 16


def sort_list(rows_ref, count, clusters, meta, base, cnt, start, index_of):
    perm, index, keep, end = base, base + count, base + 2 * count, base + 3 * count

    def clear(c, _):
        cnt[c] = 0
        return 0

    lax.fori_loop(0, clusters + 1, clear, 0, unroll=True)

    def tally(e, _):
        r = rows_ref[e]
        cnt[r] = cnt[r] + 1
        return 0

    lax.fori_loop(0, count, tally, 0, unroll=2)

    def prefix(c, run):
        n = cnt[c]
        cnt[c] = run
        start[c] = run
        meta[end + c] = jnp.where(n > 0, run + n - 1, count)
        return run + n

    lax.fori_loop(0, clusters + 1, prefix, 0, unroll=3)

    def place(e, _):
        r = rows_ref[e]
        pos = cnt[r]
        cnt[r] = pos + 1
        meta[perm + pos] = e
        meta[index + pos] = index_of(e)
        meta[keep + pos] = jnp.where(pos == start[r], 0, 1)
        return 0

    lax.fori_loop(0, count, place, 0, unroll=2)
    return end + clusters + 1


def prepare(clusters, owners, near_rows, near_sources, far_rows, far_sources, meta, asks, cnt, start, seen):
    owner = lax.axis_index("panels")
    near, far = near_rows.shape[0], far_rows.shape[0]
    first = owner * clusters - REACH

    def near_index(e):
        return near_sources[e] - first

    base = sort_list(near_rows, near, clusters, meta, 0, cnt, start, near_index)

    def clear(q, _):
        seen[q] = 0
        return 0

    lax.fori_loop(0, owners, clear, 0, unroll=True)

    def far_index(e):
        source = far_sources[e]
        target = source // clusters
        within = source - target * clusters
        slot = seen[target]
        seen[target] = slot + 1
        asks[target, 0, slot] = within
        return jnp.where(
            target == owner, within + REACH, clusters + 2 * REACH + CAPACITY * target + slot
        )

    sort_list(far_rows, far, clusters, meta, base, cnt, start, far_index)


def permute(source, index_ref, clusters, emit):
    def group(t, _):
        index = jnp.broadcast_to(index_ref[pl.ds(t, 1), :], (ROWS, 128))
        low, high = index & 127, index >> 7
        tile = jnp.zeros((ROWS, 128), jnp.float32)
        for s in range(clusters):
            moved = jnp.take_along_axis(source[s], low, axis=1, mode="promise_in_bounds")
            tile = jnp.where(high == s, moved, tile)
        emit(t, tile)
        return 0

    lax.fori_loop(0, clusters, group, 0)


def kernel(
    clusters,
    owners,
    shares,
    near,
    far,
    incident,
    order,
    asks,
    meta,
    near_hbm,
    far_left,
    far_right,
    first_image,
    second_image,
    blocks,
    values,
    local,
    inverse,
    own_a,
    own_b,
    table_a,
    table_b,
    stage_a,
    stage_b,
    near_sums,
    far_sums,
    send_a,
    send_b,
    recv_a,
    recv_b,
    asked_v,
    asked_s,
    squares,
    all_squares,
    load_sem,
    asked_sem,
    ask_send,
    ask_recv,
    seg_send,
    seg_recv,
    halo_send,
    halo_recv,
    half_send,
    half_recv,
    sum_send,
    sum_recv,
    sq_send,
    sq_recv,
):
    p = lax.axis_index("panels")
    r = lax.axis_index("rhs")
    span = clusters // CHUNKS
    slots = clusters + 2 * REACH

    load = pltpu.make_async_copy(near_hbm, blocks, load_sem)
    load.start()

    def peers(body):
        def step(j, _):
            q = lax.rem(p + j, owners)
            for s in range(shares):
                body(q, s)
            return 0

        lax.fori_loop(1, owners, step, 0)

    def others(body):
        for j in range(1, shares):
            body(lax.rem(r + j, shares))

    barrier = pltpu.get_barrier_semaphore()

    def greet(q, s):
        pl.semaphore_signal(
            barrier, inc=1, device_id={"panels": q, "rhs": s}, device_id_type=MESH
        )

    peers(greet)
    others(lambda s: greet(p, s))

    asked_v[p] = jnp.zeros_like(asked_v[p])
    for s in range(clusters):
        values[s] = incident[:, s * 128 : (s + 1) * 128].astype(jnp.float32)
    local[...] = order[...] - p * (clusters * 128)
    near_sums[near] = jnp.zeros_like(near_sums[near])
    far_sums[far] = jnp.zeros_like(far_sums[far])

    pl.semaphore_wait(barrier, shares * owners - 1)

    def ask_copy(q, s, src_owner, src_rhs):
        return pltpu.make_async_remote_copy(
            src_ref=asks.at[q],
            dst_ref=asked_v.at[src_owner, src_rhs],
            send_sem=ask_send.at[q, s],
            recv_sem=ask_recv.at[src_owner, src_rhs],
            device_id={"panels": q, "rhs": s},
            device_id_type=MESH,
        )

    peers(lambda q, s: ask_copy(q, s, p, r).start())

    def half_copy(phase, own, table, k, s, src_rhs):
        return pltpu.make_async_remote_copy(
            src_ref=own.at[pl.ds(k * span, span)],
            dst_ref=table.at[pl.ds(REACH + k * span, span), src_rhs],
            send_sem=half_send.at[phase, k, s],
            recv_sem=half_recv.at[phase, k, src_rhs],
            device_id={"panels": p, "rhs": s},
            device_id_type=MESH,
        )

    def seg_copy(phase, stage, table, q, s, src_owner, src_rhs):
        return pltpu.make_async_remote_copy(
            src_ref=stage.at[q, s],
            dst_ref=table.at[pl.ds(slots + CAPACITY * src_owner, CAPACITY), src_rhs],
            send_sem=seg_send.at[phase, q, s],
            recv_sem=seg_recv.at[phase, src_owner, src_rhs],
            device_id={"panels": q, "rhs": s},
            device_id_type=MESH,
        )

    def halo_copy(phase, own, table, up, q, s, src_rhs):
        src, dst = (clusters - REACH, 0) if up else (0, clusters + REACH)
        side = 0 if up else 1
        return pltpu.make_async_remote_copy(
            src_ref=own.at[pl.ds(src, REACH)],
            dst_ref=table.at[pl.ds(dst, REACH), src_rhs],
            send_sem=halo_send.at[phase, side, s],
            recv_sem=halo_recv.at[phase, side, src_rhs],
            device_id={"panels": q, "rhs": s},
            device_id_type=MESH,
        )

    has_next, has_last = p < owners - 1, p > 0

    def halos(phase, own, table, act):
        @pl.when(has_next)
        def _():
            for s in range(shares):
                act(halo_copy(phase, own, table, True, p + 1, s, r), True)

        @pl.when(has_last)
        def _():
            for s in range(shares):
                act(halo_copy(phase, own, table, False, p - 1, s, r), False)

    def spread(phase, own, table, stage):
        halos(phase, own, table, lambda copy, _: copy.start())

        def serve(q, s):
            for k in range(CAPACITY):
                stage[q, s, k] = own[asked_s[q, s, 0, k]]
            seg_copy(phase, stage, table, q, s, p, r).start()

        peers(serve)

    def gathered(phase, own, table, stage):
        for k in range(CHUNKS):
            others(lambda s: half_copy(phase, own, table, k, s, s).wait_recv())

        @pl.when(has_last)
        def _():
            for s in range(shares):
                halo_copy(phase, own, table, True, p, s, s).wait_recv()

        @pl.when(has_next)
        def _():
            for s in range(shares):
                halo_copy(phase, own, table, False, p, s, s).wait_recv()

        peers(lambda q, s: seg_copy(phase, stage, table, q, s, q, s).wait_recv())

    def sent(phase, own, table, stage):
        for k in range(CHUNKS):
            others(lambda s: half_copy(phase, own, table, k, s, r).wait_send())
        halos(phase, own, table, lambda copy, _: copy.wait_send())
        peers(lambda q, s: seg_copy(phase, stage, table, q, s, p, r).wait_send())

    base = 3 * near + clusters + 1

    def apply(table):
        def near_step(i, acc):
            segment = table[meta[near + i]].reshape(shares * ROWS, 128)
            block = blocks[meta[i]]
            term = lax.dot_general(segment, block, LAST, preferred_element_type=jnp.float32)
            acc = acc * meta[2 * near + i].astype(jnp.float32) + term
            near_sums[i] = acc.reshape(shares, ROWS, 128)
            return acc

        def far_step(i, acc):
            segment = table[meta[base + far + i]].reshape(shares * ROWS, 128)
            entry = meta[base + i]
            coefficients = lax.dot_general(
                segment, far_right[entry], LAST, preferred_element_type=jnp.float32
            ).astype(jnp.bfloat16)
            term = jnp.dot(coefficients, far_left[entry], preferred_element_type=jnp.float32)
            acc = acc * meta[base + 2 * far + i].astype(jnp.float32) + term
            far_sums[i] = acc.reshape(shares, ROWS, 128)
            return acc

        zero = jnp.zeros((shares * ROWS, 128), jnp.float32)
        lax.fori_loop(0, far, far_step, zero, unroll=4 if shares > 2 else far)
        lax.fori_loop(0, near, near_step, zero, unroll=16)

    def part(c, s):
        return (
            near_sums[meta[3 * near + c], s] + far_sums[meta[base + 3 * far + c], s]
        )

    def sum_copy(phase, send, recv, k, s, src_rhs):
        return pltpu.make_async_remote_copy(
            src_ref=send.at[s, pl.ds(k * span, span)],
            dst_ref=recv.at[src_rhs, pl.ds(k * span, span)],
            send_sem=sum_send.at[phase, k, s],
            recv_sem=sum_recv.at[phase, k, src_rhs],
            device_id={"panels": p, "rhs": s},
            device_id_type=MESH,
        )

    def reduce(phase, send, recv, take, after):
        def give(k, s):
            for c in range(k * span, (k + 1) * span):
                send[s, c] = part(c, s)
            sum_copy(phase, send, recv, k, s, r).start()

        for k in range(CHUNKS):
            others(lambda s: give(k, s))
        for k in range(CHUNKS):
            others(lambda s: sum_copy(phase, send, recv, k, s, s).wait_recv())
            for c in range(k * span, (k + 1) * span):
                tile = part(c, r)
                for j in range(1, shares):
                    tile = tile + recv[lax.rem(r + j, shares), c]
                take(c, tile)
            after(k)

    def tree_tile(t, tile):
        tile = tile.astype(jnp.bfloat16)
        own_a[t] = tile
        table_a[REACH + t, r] = tile

    permute(values, local, clusters, tree_tile)
    for k in range(CHUNKS):
        others(lambda s: half_copy(0, own_a, table_a, k, s, r).start())
    peers(lambda q, s: ask_copy(q, s, q, s).wait_recv())
    to_scalar = pltpu.make_async_copy(asked_v, asked_s, asked_sem)
    to_scalar.start()
    to_scalar.wait()
    spread(0, own_a, table_a, stage_a)

    digits = jnp.zeros((2 * clusters, 128), jnp.float32)
    lane = lax.broadcasted_iota(jnp.int32, (1, 128), 1)
    for s in range(clusters):
        row = local[s : s + 1, :]
        groups = lax.broadcasted_iota(jnp.int32, (clusters, 128), 0) == (row >> 7)
        position = lane + s * 128
        top = jnp.where(groups, (position >> 6).astype(jnp.float32), 0.0)
        bottom = jnp.where(groups, (position & 63).astype(jnp.float32), 0.0)
        left = jnp.concatenate([top, bottom], axis=0).astype(jnp.bfloat16)
        hot = lax.broadcasted_iota(jnp.int32, (128, 128), 0) == (row & 127)
        hot = jnp.where(hot, 1.0, 0.0).astype(jnp.bfloat16)
        digits = digits + lax.dot_general(left, hot, LAST, preferred_element_type=jnp.float32)
    inverse[...] = (digits[:clusters] * 64.0 + digits[clusters:]).astype(jnp.int32)

    load.wait()
    gathered(0, own_a, table_a, stage_a)
    apply(table_a)

    squares[...] = jnp.zeros_like(squares)

    def first_tile(c, tile):
        values[c] = tile
        squares[...] += tile * tile
        tile = tile.astype(jnp.bfloat16)
        own_b[c] = tile
        table_b[REACH + c, r] = tile

    def share(k):
        others(lambda s: half_copy(1, own_b, table_b, k, s, r).start())

    reduce(0, send_a, recv_a, first_tile, share)
    spread(1, own_b, table_b, stage_b)

    def sq_copy(q, src_owner):
        return pltpu.make_async_remote_copy(
            src_ref=squares,
            dst_ref=all_squares.at[src_owner],
            send_sem=sq_send.at[q],
            recv_sem=sq_recv.at[src_owner],
            device_id={"panels": q, "rhs": r},
            device_id_type=MESH,
        )

    def same(body):
        def step(j, _):
            body(lax.rem(p + j, owners))
            return 0

        lax.fori_loop(1, owners, step, 0)

    same(lambda q: sq_copy(q, p).start())
    all_squares[p] = squares[...]

    def first_out(t, tile):
        first_image[:, pl.ds(pl.multiple_of(t * 128, 128), 128)] = tile

    permute(values, inverse, clusters, first_out)

    gathered(1, own_b, table_b, stage_b)
    apply(table_b)
    same(lambda q: sq_copy(q, q).wait_recv())
    total = lax.fori_loop(
        0, owners, lambda q, acc: acc + all_squares[q], jnp.zeros((ROWS, 128), jnp.float32)
    )
    total = jnp.sum(total, axis=1, keepdims=True)
    scale = lax.rsqrt(total / (clusters * 128 * owners) + 1e-06)

    def second_tile(c, tile):
        values[c] = tile * scale

    reduce(1, send_b, recv_b, second_tile, lambda k: None)

    def second_out(t, tile):
        second_image[:, pl.ds(pl.multiple_of(t * 128, 128), 128)] = tile

    permute(values, inverse, clusters, second_out)

    peers(lambda q, s: ask_copy(q, s, p, r).wait_send())
    sent(0, own_a, table_a, stage_a)
    sent(1, own_b, table_b, stage_b)
    for k in range(CHUNKS):
        others(lambda s: sum_copy(0, send_a, recv_a, k, s, r).wait_send())
        others(lambda s: sum_copy(1, send_b, recv_b, k, s, r).wait_send())
    same(lambda q: sq_copy(q, p).wait_send())


def on_device(
    owners,
    shares,
    incident,
    tree_order,
    near_rows,
    near_sources,
    near_blocks,
    far_rows,
    far_sources,
    far_left,
    far_right,
):
    headings, panels = incident.shape
    incident = jnp.pad(incident, ((0, ROWS - headings), (0, 0)))
    near, block = near_blocks.shape[:2]
    far, rank = far_left.shape[:2]
    clusters = panels // block
    slots = clusters + 2 * REACH + CAPACITY * owners
    smem = pl.BlockSpec(memory_space=pltpu.SMEM)
    vmem = pl.BlockSpec(memory_space=pltpu.VMEM)
    meta_size = 3 * (near + far) + 2 * (clusters + 1)
    meta, asks = pl.pallas_call(
        functools.partial(prepare, clusters, owners),
        out_shape=(
            jax.ShapeDtypeStruct((meta_size,), jnp.int32),
            jax.ShapeDtypeStruct((owners, 1, 128), jnp.int32),
        ),
        in_specs=[smem] * 4,
        out_specs=(smem, smem),
        scratch_shapes=[
            pltpu.SMEM((clusters + 1,), jnp.int32),
            pltpu.SMEM((clusters + 1,), jnp.int32),
            pltpu.SMEM((owners,), jnp.int32),
        ],
    )(near_rows, near_sources, far_rows, far_sources)
    bf, f32 = jnp.bfloat16, jnp.float32
    dma = pltpu.SemaphoreType.DMA
    image = jax.ShapeDtypeStruct((ROWS, panels), f32)
    first, second = pl.pallas_call(
        functools.partial(kernel, clusters, owners, shares, near, far),
        out_shape=(image, image),
        in_specs=[vmem, vmem, vmem, smem, pl.BlockSpec(memory_space=pl.ANY), vmem, vmem],
        out_specs=(vmem, vmem),
        scratch_shapes=[
            pltpu.VMEM((near, block, block), bf),
            pltpu.VMEM((clusters, ROWS, block), f32),
            pltpu.VMEM((clusters, block), jnp.int32),
            pltpu.VMEM((clusters, block), jnp.int32),
            pltpu.VMEM((clusters, ROWS, block), bf),
            pltpu.VMEM((clusters, ROWS, block), bf),
            pltpu.VMEM((slots, shares, ROWS, block), bf),
            pltpu.VMEM((slots, shares, ROWS, block), bf),
            pltpu.VMEM((owners, shares, CAPACITY, ROWS, block), bf),
            pltpu.VMEM((owners, shares, CAPACITY, ROWS, block), bf),
            pltpu.VMEM((near + 1, shares, ROWS, block), f32),
            pltpu.VMEM((far + 1, shares, ROWS, block), f32),
            pltpu.VMEM((shares, clusters, ROWS, block), f32),
            pltpu.VMEM((shares, clusters, ROWS, block), f32),
            pltpu.VMEM((shares, clusters, ROWS, block), f32),
            pltpu.VMEM((shares, clusters, ROWS, block), f32),
            pltpu.VMEM((owners, shares, 1, 128), jnp.int32),
            pltpu.SMEM((owners, shares, 1, 128), jnp.int32),
            pltpu.VMEM((ROWS, block), f32),
            pltpu.VMEM((owners, ROWS, block), f32),
            dma,
            dma,
            dma((owners, shares)),
            dma((owners, shares)),
            dma((2, owners, shares)),
            dma((2, owners, shares)),
            dma((2, 2, shares)),
            dma((2, 2, shares)),
            dma((2, CHUNKS, shares)),
            dma((2, CHUNKS, shares)),
            dma((2, CHUNKS, shares)),
            dma((2, CHUNKS, shares)),
            dma((owners,)),
            dma((owners,)),
        ],
        compiler_params=pltpu.CompilerParams(
            collective_id=0, has_side_effects=True, vmem_limit_bytes=56 * 2**20
        ),
    )(
        incident,
        tree_order.reshape(clusters, block),
        asks,
        meta,
        near_blocks,
        far_left,
        far_right,
    )
    return first[:headings], second[:headings]


def solution(mesh):
    lists = ("groups", "panels", "rhs")
    in_specs = (
        P("rhs", ("groups", "panels")),
        P(("groups", "panels")),
        P(lists),
        P(lists),
        P(lists, None, None),
        P(lists),
        P(lists),
        P(lists, None, None),
        P(lists, None, None),
    )
    out_specs = (P("rhs", ("groups", "panels")), P("rhs", ("groups", "panels")))
    return jax.shard_map(
        functools.partial(on_device, mesh.shape["panels"], mesh.shape["rhs"]),
        mesh=mesh,
        in_specs=in_specs,
        out_specs=out_specs,
        check_vma=False,
    )
```

```python
import functools

import jax
import jax.numpy as jnp
from jax import lax
from jax.experimental import pallas as pl
from jax.experimental.pallas import tpu as pltpu
from jax.sharding import PartitionSpec as P

MESH = pl.DeviceIdType.MESH
REACH = 2
CAPACITY = 2
LAST = (((1,), (1,)), ((), ()))
CHUNKS = 4
ROWS = 16


def sort_list(rows_ref, count, clusters, meta, base, cnt, start, index_of):
    perm, index, keep, end = base, base + count, base + 2 * count, base + 3 * count

    def clear(c, _):
        cnt[c] = 0
        return 0

    lax.fori_loop(0, clusters + 1, clear, 0, unroll=True)

    def tally(e, _):
        r = rows_ref[e]
        cnt[r] = cnt[r] + 1
        return 0

    lax.fori_loop(0, count, tally, 0, unroll=2)

    def prefix(c, run):
        n = cnt[c]
        cnt[c] = run
        start[c] = run
        meta[end + c] = jnp.where(n > 0, run + n - 1, count)
        return run + n

    lax.fori_loop(0, clusters + 1, prefix, 0, unroll=3)

    def place(e, _):
        r = rows_ref[e]
        pos = cnt[r]
        cnt[r] = pos + 1
        meta[perm + pos] = e
        meta[index + pos] = index_of(e)
        meta[keep + pos] = jnp.where(pos == start[r], 0, 1)
        return 0

    lax.fori_loop(0, count, place, 0, unroll=2)
    return end + clusters + 1


def prepare(clusters, owners, near_rows, near_sources, far_rows, far_sources, meta, asks, cnt, start, seen):
    owner = lax.axis_index("panels")
    near, far = near_rows.shape[0], far_rows.shape[0]
    first = owner * clusters - REACH

    def near_index(e):
        return near_sources[e] - first

    base = sort_list(near_rows, near, clusters, meta, 0, cnt, start, near_index)

    def clear(q, _):
        seen[q] = 0
        return 0

    lax.fori_loop(0, owners, clear, 0, unroll=True)

    def far_index(e):
        source = far_sources[e]
        target = source // clusters
        within = source - target * clusters
        slot = seen[target]
        seen[target] = slot + 1
        asks[target, 0, slot] = within
        return jnp.where(
            target == owner, within + REACH, clusters + 2 * REACH + CAPACITY * target + slot
        )

    sort_list(far_rows, far, clusters, meta, base, cnt, start, far_index)


def permute(source, index_ref, clusters, emit):
    for t in range(clusters):
        index = jnp.broadcast_to(index_ref[t : t + 1, :], (ROWS, 128))
        low, high = index & 127, index >> 7
        tile = jnp.zeros((ROWS, 128), jnp.float32)
        for s in range(clusters):
            moved = jnp.take_along_axis(source[s], low, axis=1, mode="promise_in_bounds")
            tile = jnp.where(high == s, moved, tile)
        emit(t, tile)


def kernel(
    clusters,
    owners,
    shares,
    near,
    far,
    incident,
    order,
    asks,
    meta,
    near_hbm,
    far_left,
    far_right,
    first_image,
    second_tree,
    inverse,
    blocks,
    values,
    local,
    own_a,
    own_b,
    table_a,
    table_b,
    stage_a,
    stage_b,
    near_sums,
    far_sums,
    send_a,
    send_b,
    recv_a,
    recv_b,
    asked_v,
    asked_s,
    squares,
    all_squares,
    load_sem,
    asked_sem,
    ask_send,
    ask_recv,
    out_sem,
    in_sem,
    sum_send,
    sum_recv,
    sq_send,
    sq_recv,
):
    p = lax.axis_index("panels")
    r = lax.axis_index("rhs")
    span = clusters // CHUNKS
    slots = clusters + 2 * REACH

    load = pltpu.make_async_copy(near_hbm, blocks, load_sem)
    load.start()

    def peers(body):
        def step(j, _):
            q = lax.rem(p + j, owners)
            for s in range(shares):
                body(q, s)
            return 0

        lax.fori_loop(1, owners, step, 0)

    def others(body):
        for j in range(1, shares):
            body(lax.rem(r + j, shares))

    barrier = pltpu.get_barrier_semaphore()

    def greet(q, s):
        pl.semaphore_signal(
            barrier, inc=1, device_id={"panels": q, "rhs": s}, device_id_type=MESH
        )

    peers(greet)
    others(lambda s: greet(p, s))

    asked_v[p] = jnp.zeros_like(asked_v[p])
    for s in range(clusters):
        values[s] = incident[:, s * 128 : (s + 1) * 128].astype(jnp.float32)
    local[...] = order[...] - p * (clusters * 128)
    near_sums[near] = jnp.zeros_like(near_sums[near])
    far_sums[far] = jnp.zeros_like(far_sums[far])

    pl.semaphore_wait(barrier, shares * owners - 1)

    def ask_copy(q, s, src_owner, src_rhs):
        return pltpu.make_async_remote_copy(
            src_ref=asks.at[q],
            dst_ref=asked_v.at[src_owner, src_rhs],
            send_sem=ask_send,
            recv_sem=ask_recv,
            device_id={"panels": q, "rhs": s},
            device_id_type=MESH,
        )

    peers(lambda q, s: ask_copy(q, s, p, r).start())

    def half_copy(phase, own, table, k, s, src_rhs):
        return pltpu.make_async_remote_copy(
            src_ref=own.at[pl.ds(k * span, span)],
            dst_ref=table.at[pl.ds(REACH + k * span, span), src_rhs],
            send_sem=out_sem.at[phase],
            recv_sem=in_sem.at[phase],
            device_id={"panels": p, "rhs": s},
            device_id_type=MESH,
        )

    def seg_copy(phase, stage, table, q, s, src_owner, src_rhs):
        return pltpu.make_async_remote_copy(
            src_ref=stage.at[q, s],
            dst_ref=table.at[pl.ds(slots + CAPACITY * src_owner, CAPACITY), src_rhs],
            send_sem=out_sem.at[phase],
            recv_sem=in_sem.at[phase],
            device_id={"panels": q, "rhs": s},
            device_id_type=MESH,
        )

    def halo_copy(phase, own, table, up, q, s, src_rhs):
        src, dst = (clusters - REACH, 0) if up else (0, clusters + REACH)
        return pltpu.make_async_remote_copy(
            src_ref=own.at[pl.ds(src, REACH)],
            dst_ref=table.at[pl.ds(dst, REACH), src_rhs],
            send_sem=out_sem.at[phase],
            recv_sem=in_sem.at[phase],
            device_id={"panels": q, "rhs": s},
            device_id_type=MESH,
        )

    def spread(phase, own, table, stage):
        for s in range(shares):
            halo_copy(phase, own, table, True, lax.rem(p + 1, owners), s, r).start()
            halo_copy(phase, own, table, False, lax.rem(p + owners - 1, owners), s, r).start()

        def serve(q, s):
            for k in range(CAPACITY):
                stage[q, s, k] = own[asked_s[q, s, 0, k]]
            seg_copy(phase, stage, table, q, s, p, r).start()

        peers(serve)

    moved = (shares - 1) * clusters // shares + (owners - 1) * CAPACITY + 2 * REACH

    def wait_bytes(view, sem):
        pltpu.make_async_copy(view, view, sem).wait()

    def gathered(phase, table):
        wait_bytes(table.at[pl.ds(0, moved)], in_sem.at[phase])

    base = 3 * near + clusters + 1

    def apply(table):
        def far_step(i, acc):
            segment = table[meta[base + far + i]].reshape(shares * ROWS, 128)
            entry = meta[base + i]
            coefficients = lax.dot_general(
                segment, far_right[entry], LAST, preferred_element_type=jnp.float32
            ).astype(jnp.bfloat16)
            term = jnp.dot(coefficients, far_left[entry], preferred_element_type=jnp.float32)
            acc = acc * meta[base + 2 * far + i].astype(jnp.float32) + term
            far_sums[i] = acc.reshape(shares, ROWS, 128)
            return acc

        rows = shares * ROWS
        group = 2 if near % 2 == 0 else 1

        def near_step(g, acc):
            places = [g * group + k for k in range(group)]
            segments = [table[meta[near + i]].reshape(rows, 128) for i in places]
            weights = [blocks[meta[i]] for i in places]
            terms = lax.dot_general(
                jnp.concatenate(segments, axis=0),
                jnp.concatenate(weights, axis=0),
                LAST,
                preferred_element_type=jnp.float32,
            )
            for k, i in enumerate(places):
                term = terms[k * rows : (k + 1) * rows, k * 128 : (k + 1) * 128]
                acc = acc * meta[2 * near + i].astype(jnp.float32) + term
                near_sums[i] = acc.reshape(shares, ROWS, 128)
            return acc

        zero = jnp.zeros((rows, 128), jnp.float32)
        steps = near // group
        lax.fori_loop(0, far, far_step, zero, unroll=far if shares <= 2 else 2)
        lax.fori_loop(0, steps, near_step, zero, unroll=steps if shares <= 2 else 2)

    def part(c, s):
        return (
            near_sums[meta[3 * near + c], s] + far_sums[meta[base + 3 * far + c], s]
        )

    def sum_copy(phase, send, recv, k, s, src_rhs):
        return pltpu.make_async_remote_copy(
            src_ref=send.at[s, pl.ds(k * span, span)],
            dst_ref=recv.at[src_rhs, pl.ds(k * span, span)],
            send_sem=sum_send.at[phase],
            recv_sem=sum_recv.at[phase, k, src_rhs],
            device_id={"panels": p, "rhs": s},
            device_id_type=MESH,
        )

    def reduce(phase, send, recv, take, after):
        def give(k, s):
            for c in range(k * span, (k + 1) * span):
                send[s, c] = part(c, s).astype(jnp.bfloat16)
            sum_copy(phase, send, recv, k, s, r).start()

        for k in range(CHUNKS):
            others(lambda s: give(k, s))
        for k in range(CHUNKS):
            others(lambda s: sum_copy(phase, send, recv, k, s, s).wait_recv())
            for c in range(k * span, (k + 1) * span):
                tile = part(c, r)
                for j in range(1, shares):
                    tile = tile + recv[lax.rem(r + j, shares), c]
                take(c, tile)
            after(k)

    def tree_tile(t, tile):
        tile = tile.astype(jnp.bfloat16)
        own_a[t] = tile
        table_a[REACH + t, r] = tile

    permute(values, local, clusters, tree_tile)
    for k in range(CHUNKS):
        others(lambda s: half_copy(0, own_a, table_a, k, s, r).start())
    wait_bytes(asked_v.at[pl.ds(0, owners - 1)], ask_recv)
    to_scalar = pltpu.make_async_copy(asked_v, asked_s, asked_sem)
    to_scalar.start()
    to_scalar.wait()
    spread(0, own_a, table_a, stage_a)

    digits = jnp.zeros((2 * clusters, 128), jnp.float32)
    lane = lax.broadcasted_iota(jnp.int32, (1, 128), 1)
    for s in range(clusters):
        row = local[s : s + 1, :]
        groups = lax.broadcasted_iota(jnp.int32, (clusters, 128), 0) == (row >> 7)
        position = lane + s * 128
        top = jnp.where(groups, (position >> 6).astype(jnp.float32), 0.0)
        bottom = jnp.where(groups, (position & 63).astype(jnp.float32), 0.0)
        left = jnp.concatenate([top, bottom], axis=0).astype(jnp.bfloat16)
        hot = lax.broadcasted_iota(jnp.int32, (128, 128), 0) == (row & 127)
        hot = jnp.where(hot, 1.0, 0.0).astype(jnp.bfloat16)
        digits = digits + lax.dot_general(left, hot, LAST, preferred_element_type=jnp.float32)
    inverse[...] = (digits[:clusters] * 64.0 + digits[clusters:]).astype(jnp.int32)

    load.wait()
    gathered(0, table_a)
    apply(table_a)

    squares[...] = jnp.zeros_like(squares)

    def first_tile(c, tile):
        values[c] = tile
        squares[...] += tile * tile
        tile = tile.astype(jnp.bfloat16)
        own_b[c] = tile
        table_b[REACH + c, r] = tile

    def share(k):
        others(lambda s: half_copy(1, own_b, table_b, k, s, r).start())

    reduce(0, send_a, recv_a, first_tile, share)
    spread(1, own_b, table_b, stage_b)

    def sq_copy(q, src_owner):
        return pltpu.make_async_remote_copy(
            src_ref=squares,
            dst_ref=all_squares.at[src_owner],
            send_sem=sq_send,
            recv_sem=sq_recv,
            device_id={"panels": q, "rhs": r},
            device_id_type=MESH,
        )

    def same(body):
        def step(j, _):
            body(lax.rem(p + j, owners))
            return 0

        lax.fori_loop(1, owners, step, 0)

    same(lambda q: sq_copy(q, p).start())
    all_squares[p] = squares[...]

    def first_out(t, tile):
        first_image[:, t * 128 : (t + 1) * 128] = tile

    permute(values, inverse, clusters, first_out)

    gathered(1, table_b)
    apply(table_b)
    wait_bytes(all_squares.at[pl.ds(0, owners - 1)], sq_recv)
    total = lax.fori_loop(
        0, owners, lambda q, acc: acc + all_squares[q], jnp.zeros((ROWS, 128), jnp.float32)
    )
    total = jnp.sum(total, axis=1, keepdims=True)
    scale = lax.rsqrt(total / (clusters * 128 * owners) + 1e-06)

    def second_tile(c, tile):
        second_tree[c] = tile * scale

    reduce(1, send_b, recv_b, second_tile, lambda k: None)

    wait_bytes(asked_v.at[pl.ds(0, owners - 1)], ask_send)
    wait_bytes(table_a.at[pl.ds(0, moved)], out_sem.at[0])
    wait_bytes(table_b.at[pl.ds(0, moved)], out_sem.at[1])
    wait_bytes(send_a.at[pl.ds(0, shares - 1)], sum_send.at[0])
    wait_bytes(send_b.at[pl.ds(0, shares - 1)], sum_send.at[1])
    wait_bytes(all_squares.at[pl.ds(0, owners - 1)], sq_send)


def finish(clusters, first_tree, second_tree, inverse, first_image, second_image, sem):
    copy = pltpu.make_async_copy(first_tree, first_image, sem)
    copy.start()

    def emit(t, tile):
        second_image[:, t * 128 : (t + 1) * 128] = tile

    permute(second_tree, inverse, clusters, emit)
    copy.wait()


def on_device(
    owners,
    shares,
    incident,
    tree_order,
    near_rows,
    near_sources,
    near_blocks,
    far_rows,
    far_sources,
    far_left,
    far_right,
):
    headings, panels = incident.shape
    incident = jnp.pad(incident, ((0, ROWS - headings), (0, 0)))
    near, block = near_blocks.shape[:2]
    far, rank = far_left.shape[:2]
    clusters = panels // block
    slots = clusters + 2 * REACH + CAPACITY * owners
    smem = pl.BlockSpec(memory_space=pltpu.SMEM)
    vmem = pl.BlockSpec(memory_space=pltpu.VMEM)
    meta_size = 3 * (near + far) + 2 * (clusters + 1)
    meta, asks = pl.pallas_call(
        functools.partial(prepare, clusters, owners),
        out_shape=(
            jax.ShapeDtypeStruct((meta_size,), jnp.int32),
            jax.ShapeDtypeStruct((owners, 1, 128), jnp.int32),
        ),
        in_specs=[smem] * 4,
        out_specs=(smem, smem),
        scratch_shapes=[
            pltpu.SMEM((clusters + 1,), jnp.int32),
            pltpu.SMEM((clusters + 1,), jnp.int32),
            pltpu.SMEM((owners,), jnp.int32),
        ],
    )(near_rows, near_sources, far_rows, far_sources)
    bf, f32 = jnp.bfloat16, jnp.float32
    dma = pltpu.SemaphoreType.DMA
    image = jax.ShapeDtypeStruct((ROWS, panels), f32)
    first, second, inverse = pl.pallas_call(
        functools.partial(kernel, clusters, owners, shares, near, far),
        out_shape=(
            image,
            jax.ShapeDtypeStruct((clusters, ROWS, block), f32),
            jax.ShapeDtypeStruct((clusters, block), jnp.int32),
        ),
        in_specs=[vmem, vmem, vmem, smem, pl.BlockSpec(memory_space=pl.ANY), vmem, vmem],
        out_specs=(vmem, vmem, vmem),
        scratch_shapes=[
            pltpu.VMEM((near, block, block), bf),
            pltpu.VMEM((clusters, ROWS, block), f32),
            pltpu.VMEM((clusters, block), jnp.int32),
            pltpu.VMEM((clusters, ROWS, block), bf),
            pltpu.VMEM((clusters, ROWS, block), bf),
            pltpu.VMEM((slots, shares, ROWS, block), bf),
            pltpu.VMEM((slots, shares, ROWS, block), bf),
            pltpu.VMEM((owners, shares, CAPACITY, ROWS, block), bf),
            pltpu.VMEM((owners, shares, CAPACITY, ROWS, block), bf),
            pltpu.VMEM((near + 1, shares, ROWS, block), f32),
            pltpu.VMEM((far + 1, shares, ROWS, block), f32),
            pltpu.VMEM((shares, clusters, ROWS, block), bf),
            pltpu.VMEM((shares, clusters, ROWS, block), bf),
            pltpu.VMEM((shares, clusters, ROWS, block), bf),
            pltpu.VMEM((shares, clusters, ROWS, block), bf),
            pltpu.VMEM((owners, shares, 1, 128), jnp.int32),
            pltpu.SMEM((owners, shares, 1, 128), jnp.int32),
            pltpu.VMEM((ROWS, block), f32),
            pltpu.VMEM((owners, ROWS, block), f32),
            dma,
            dma,
            dma,
            dma,
            dma((2,)),
            dma((2,)),
            dma((2,)),
            dma((2, CHUNKS, shares)),
            dma,
            dma,
        ],
        compiler_params=pltpu.CompilerParams(
            collective_id=0, has_side_effects=True, vmem_limit_bytes=56 * 2**20
        ),
    )(
        incident,
        tree_order.reshape(clusters, block),
        asks,
        meta,
        near_blocks,
        far_left,
        far_right,
    )
    anywhere = pl.BlockSpec(memory_space=pl.ANY)
    first, second = pl.pallas_call(
        functools.partial(finish, clusters),
        out_shape=(image, image),
        in_specs=[anywhere, vmem, vmem],
        out_specs=(anywhere, vmem),
        scratch_shapes=[dma],
    )(first, second, inverse)
    return first[:headings], second[:headings]


def solution(mesh):
    lists = ("groups", "panels", "rhs")
    in_specs = (
        P("rhs", ("groups", "panels")),
        P(("groups", "panels")),
        P(lists),
        P(lists),
        P(lists, None, None),
        P(lists),
        P(lists),
        P(lists, None, None),
        P(lists, None, None),
    )
    out_specs = (P("rhs", ("groups", "panels")), P("rhs", ("groups", "panels")))
    return jax.shard_map(
        functools.partial(on_device, mesh.shape["panels"], mesh.shape["rhs"]),
        mesh=mesh,
        in_specs=in_specs,
        out_specs=out_specs,
        check_vma=False,
    )
```

```python
import functools

import jax
import jax.numpy as jnp
from jax import lax
from jax.experimental import pallas as pl
from jax.experimental.pallas import tpu as pltpu
from jax.sharding import PartitionSpec as P

MESH = pl.DeviceIdType.MESH
REACH = 2
CAPACITY = 2
LAST = (((1,), (1,)), ((), ()))
CHUNKS = 4
ROWS = 16


def sort_list(rows_ref, count, clusters, meta, base, cnt, start, index_of):
    perm, index, keep, end = base, base + count, base + 2 * count, base + 3 * count

    def clear(c, _):
        cnt[c] = 0
        return 0

    lax.fori_loop(0, clusters + 1, clear, 0, unroll=True)

    def tally(e, _):
        r = rows_ref[e]
        cnt[r] = cnt[r] + 1
        return 0

    lax.fori_loop(0, count, tally, 0, unroll=2)

    def prefix(c, run):
        n = cnt[c]
        cnt[c] = run
        start[c] = run
        meta[end + c] = jnp.where(n > 0, run + n - 1, count)
        return run + n

    lax.fori_loop(0, clusters + 1, prefix, 0, unroll=3)

    def place(e, _):
        r = rows_ref[e]
        pos = cnt[r]
        cnt[r] = pos + 1
        meta[perm + pos] = e
        meta[index + pos] = index_of(e)
        meta[keep + pos] = jnp.where(pos == start[r], 0, 1)
        return 0

    lax.fori_loop(0, count, place, 0, unroll=2)
    return end + clusters + 1


def prepare(clusters, owners, near_rows, near_sources, far_rows, far_sources, meta, asks, cnt, start, seen):
    owner = lax.axis_index("panels")
    near, far = near_rows.shape[0], far_rows.shape[0]
    first = owner * clusters - REACH

    def near_index(e):
        return near_sources[e] - first

    base = sort_list(near_rows, near, clusters, meta, 0, cnt, start, near_index)

    def clear(q, _):
        seen[q] = 0
        return 0

    lax.fori_loop(0, owners, clear, 0, unroll=True)

    def far_index(e):
        source = far_sources[e]
        target = source // clusters
        within = source - target * clusters
        slot = seen[target]
        seen[target] = slot + 1
        asks[target, 0, slot] = within
        return jnp.where(
            target == owner, within + REACH, clusters + 2 * REACH + CAPACITY * target + slot
        )

    sort_list(far_rows, far, clusters, meta, base, cnt, start, far_index)


def permute(source, index_ref, clusters, emit):
    for t in range(clusters):
        index = jnp.broadcast_to(index_ref[t : t + 1, :], (ROWS, 128))
        low, high = index & 127, index >> 7
        tile = jnp.zeros((ROWS, 128), jnp.float32)
        for s in range(clusters):
            moved = jnp.take_along_axis(source[s], low, axis=1, mode="promise_in_bounds")
            tile = jnp.where(high == s, moved, tile)
        emit(t, tile)


def kernel(
    clusters,
    owners,
    shares,
    near,
    far,
    incident,
    order,
    asks,
    meta,
    near_hbm,
    far_left,
    far_right,
    first_image,
    second_tree,
    inverse,
    blocks,
    values,
    local,
    own_a,
    own_b,
    table_a,
    table_b,
    stage_a,
    stage_b,
    near_sums,
    far_sums,
    send_a,
    send_b,
    recv_a,
    recv_b,
    asked_v,
    asked_s,
    squares,
    all_squares,
    load_sem,
    asked_sem,
    ask_send,
    ask_recv,
    out_sem,
    in_sem,
    sum_send,
    sum_recv,
    sq_send,
    sq_recv,
):
    p = lax.axis_index("panels")
    r = lax.axis_index("rhs")
    span = clusters // CHUNKS
    slots = clusters + 2 * REACH

    load = pltpu.make_async_copy(near_hbm, blocks, load_sem)
    load.start()

    def peers(body):
        def step(j, _):
            q = lax.rem(p + j, owners)
            for s in range(shares):
                body(q, s)
            return 0

        lax.fori_loop(1, owners, step, 0)

    def others(body):
        for j in range(1, shares):
            body(lax.rem(r + j, shares))

    barrier = pltpu.get_barrier_semaphore()

    def greet(q, s):
        pl.semaphore_signal(
            barrier, inc=1, device_id={"panels": q, "rhs": s}, device_id_type=MESH
        )

    peers(greet)
    others(lambda s: greet(p, s))

    asked_v[p] = jnp.zeros_like(asked_v[p])
    for s in range(clusters):
        values[s] = incident[:, s * 128 : (s + 1) * 128].astype(jnp.float32)
    local[...] = order[...] - p * (clusters * 128)
    near_sums[near] = jnp.zeros_like(near_sums[near])
    far_sums[far] = jnp.zeros_like(far_sums[far])

    pl.semaphore_wait(barrier, shares * owners - 1)

    def ask_copy(q, s, src_owner, src_rhs):
        return pltpu.make_async_remote_copy(
            src_ref=asks.at[q],
            dst_ref=asked_v.at[src_owner, src_rhs],
            send_sem=ask_send,
            recv_sem=ask_recv,
            device_id={"panels": q, "rhs": s},
            device_id_type=MESH,
        )

    peers(lambda q, s: ask_copy(q, s, p, r).start())

    def half_copy(phase, own, table, k, s, src_rhs):
        return pltpu.make_async_remote_copy(
            src_ref=own.at[pl.ds(k * span, span)],
            dst_ref=table.at[pl.ds(REACH + k * span, span), src_rhs],
            send_sem=out_sem.at[phase],
            recv_sem=in_sem.at[phase],
            device_id={"panels": p, "rhs": s},
            device_id_type=MESH,
        )

    def seg_copy(phase, stage, table, q, s, src_owner, src_rhs):
        return pltpu.make_async_remote_copy(
            src_ref=stage.at[q, s],
            dst_ref=table.at[pl.ds(slots + CAPACITY * src_owner, CAPACITY), src_rhs],
            send_sem=out_sem.at[phase],
            recv_sem=in_sem.at[phase],
            device_id={"panels": q, "rhs": s},
            device_id_type=MESH,
        )

    def halo_copy(phase, own, table, up, q, s, src_rhs):
        src, dst = (clusters - REACH, 0) if up else (0, clusters + REACH)
        return pltpu.make_async_remote_copy(
            src_ref=own.at[pl.ds(src, REACH)],
            dst_ref=table.at[pl.ds(dst, REACH), src_rhs],
            send_sem=out_sem.at[phase],
            recv_sem=in_sem.at[phase],
            device_id={"panels": q, "rhs": s},
            device_id_type=MESH,
        )

    def spread(phase, own, table, stage):
        for s in range(shares):
            halo_copy(phase, own, table, True, lax.rem(p + 1, owners), s, r).start()
            halo_copy(phase, own, table, False, lax.rem(p + owners - 1, owners), s, r).start()

        def serve(q, s):
            for k in range(CAPACITY):
                stage[q, s, k] = own[asked_s[q, s, 0, k]]
            seg_copy(phase, stage, table, q, s, p, r).start()

        peers(serve)

    moved = (shares - 1) * clusters // shares + (owners - 1) * CAPACITY + 2 * REACH

    def wait_bytes(view, sem):
        pltpu.make_async_copy(view, view, sem).wait()

    def gathered(phase, table):
        wait_bytes(table.at[pl.ds(0, moved)], in_sem.at[phase])

    base = 3 * near + clusters + 1

    def apply(table):
        def far_step(i, acc):
            segment = table[meta[base + far + i]].reshape(shares * ROWS, 128)
            entry = meta[base + i]
            coefficients = lax.dot_general(
                segment, far_right[entry], LAST, preferred_element_type=jnp.float32
            ).astype(jnp.bfloat16)
            term = jnp.dot(coefficients, far_left[entry], preferred_element_type=jnp.float32)
            acc = acc * meta[base + 2 * far + i].astype(jnp.float32) + term
            far_sums[i] = acc.reshape(shares, ROWS, 128)
            return acc

        rows = shares * ROWS
        group = 2 if near % 2 == 0 else 1

        def near_step(g, acc):
            places = [g * group + k for k in range(group)]
            segments = [table[meta[near + i]].reshape(rows, 128) for i in places]
            weights = [blocks[meta[i]] for i in places]
            terms = lax.dot_general(
                jnp.concatenate(segments, axis=0),
                jnp.concatenate(weights, axis=0),
                LAST,
                preferred_element_type=jnp.float32,
            )
            for k, i in enumerate(places):
                term = terms[k * rows : (k + 1) * rows, k * 128 : (k + 1) * 128]
                acc = acc * meta[2 * near + i].astype(jnp.float32) + term
                near_sums[i] = acc.reshape(shares, ROWS, 128)
            return acc

        zero = jnp.zeros((rows, 128), jnp.float32)
        steps = near // group
        lax.fori_loop(0, far, far_step, zero, unroll=far if shares <= 2 else 2)
        lax.fori_loop(0, steps, near_step, zero, unroll=steps if shares <= 2 else 2)

    def part(c, s):
        return (
            near_sums[meta[3 * near + c], s] + far_sums[meta[base + 3 * far + c], s]
        )

    def sum_copy(phase, send, recv, k, s, src_rhs):
        return pltpu.make_async_remote_copy(
            src_ref=send.at[s, pl.ds(k * span, span)],
            dst_ref=recv.at[src_rhs, pl.ds(k * span, span)],
            send_sem=sum_send.at[phase],
            recv_sem=sum_recv.at[phase, k, src_rhs],
            device_id={"panels": p, "rhs": s},
            device_id_type=MESH,
        )

    def reduce(phase, send, recv, take, after):
        def give(k, s):
            for c in range(k * span, (k + 1) * span):
                send[s, c] = part(c, s).astype(jnp.bfloat16)
            sum_copy(phase, send, recv, k, s, r).start()

        for k in range(CHUNKS):
            others(lambda s: give(k, s))
        for k in range(CHUNKS):
            others(lambda s: sum_copy(phase, send, recv, k, s, s).wait_recv())
            for c in range(k * span, (k + 1) * span):
                tile = part(c, r)
                for j in range(1, shares):
                    tile = tile + recv[lax.rem(r + j, shares), c]
                take(c, tile)
            after(k)

    def tree_tile(t, tile):
        tile = tile.astype(jnp.bfloat16)
        own_a[t] = tile
        table_a[REACH + t, r] = tile

    permute(values, local, clusters, tree_tile)
    for k in range(CHUNKS):
        others(lambda s: half_copy(0, own_a, table_a, k, s, r).start())
    wait_bytes(asked_v.at[pl.ds(0, owners - 1)], ask_recv)
    to_scalar = pltpu.make_async_copy(asked_v, asked_s, asked_sem)
    to_scalar.start()
    to_scalar.wait()
    spread(0, own_a, table_a, stage_a)

    digits = jnp.zeros((2 * clusters, 128), jnp.float32)
    lane = lax.broadcasted_iota(jnp.int32, (1, 128), 1)
    for s in range(clusters):
        row = local[s : s + 1, :]
        groups = lax.broadcasted_iota(jnp.int32, (clusters, 128), 0) == (row >> 7)
        position = lane + s * 128
        top = jnp.where(groups, (position >> 6).astype(jnp.float32), 0.0)
        bottom = jnp.where(groups, (position & 63).astype(jnp.float32), 0.0)
        left = jnp.concatenate([top, bottom], axis=0).astype(jnp.bfloat16)
        hot = lax.broadcasted_iota(jnp.int32, (128, 128), 0) == (row & 127)
        hot = jnp.where(hot, 1.0, 0.0).astype(jnp.bfloat16)
        digits = digits + lax.dot_general(left, hot, LAST, preferred_element_type=jnp.float32)
    inverse[...] = (digits[:clusters] * 64.0 + digits[clusters:]).astype(jnp.int32)

    load.wait()
    gathered(0, table_a)
    apply(table_a)

    squares[...] = jnp.zeros_like(squares)

    def first_tile(c, tile):
        values[c] = tile
        squares[...] += tile * tile
        tile = tile.astype(jnp.bfloat16)
        own_b[c] = tile
        table_b[REACH + c, r] = tile

    def share(k):
        others(lambda s: half_copy(1, own_b, table_b, k, s, r).start())

    reduce(0, send_a, recv_a, first_tile, share)
    spread(1, own_b, table_b, stage_b)

    def sq_copy(q, src_owner):
        return pltpu.make_async_remote_copy(
            src_ref=squares,
            dst_ref=all_squares.at[src_owner],
            send_sem=sq_send,
            recv_sem=sq_recv,
            device_id={"panels": q, "rhs": r},
            device_id_type=MESH,
        )

    def same(body):
        def step(j, _):
            body(lax.rem(p + j, owners))
            return 0

        lax.fori_loop(1, owners, step, 0)

    same(lambda q: sq_copy(q, p).start())
    all_squares[p] = squares[...]

    def first_out(t, tile):
        first_image[:, t * 128 : (t + 1) * 128] = tile

    permute(values, inverse, clusters, first_out)

    gathered(1, table_b)
    apply(table_b)
    wait_bytes(all_squares.at[pl.ds(0, owners - 1)], sq_recv)
    total = lax.fori_loop(
        0, owners, lambda q, acc: acc + all_squares[q], jnp.zeros((ROWS, 128), jnp.float32)
    )
    total = jnp.sum(total, axis=1, keepdims=True)
    scale = lax.rsqrt(total / (clusters * 128 * owners) + 1e-06)

    def second_tile(c, tile):
        second_tree[c] = tile * scale

    reduce(1, send_b, recv_b, second_tile, lambda k: None)

    wait_bytes(asked_v.at[pl.ds(0, owners - 1)], ask_send)
    wait_bytes(table_a.at[pl.ds(0, moved)], out_sem.at[0])
    wait_bytes(table_b.at[pl.ds(0, moved)], out_sem.at[1])
    wait_bytes(send_a.at[pl.ds(0, shares - 1)], sum_send.at[0])
    wait_bytes(send_b.at[pl.ds(0, shares - 1)], sum_send.at[1])
    wait_bytes(all_squares.at[pl.ds(0, owners - 1)], sq_send)


def finish(clusters, first_tree, second_tree, inverse, first_image, second_image, tiles, sems):
    first = pltpu.make_async_copy(first_tree, first_image, sems.at[CHUNKS])
    first.start()
    span = clusters // CHUNKS
    copies = []

    def emit(t, tile):
        tiles[:, t * 128 : (t + 1) * 128] = tile
        if t % span == span - 1:
            k = t // span
            columns = pl.ds(k * span * 128, span * 128)
            copies.append(
                pltpu.make_async_copy(tiles.at[:, columns], second_image.at[:, columns], sems.at[k])
            )
            copies[-1].start()

    permute(second_tree, inverse, clusters, emit)
    first.wait()
    for copy in copies:
        copy.wait()


def on_device(
    owners,
    shares,
    incident,
    tree_order,
    near_rows,
    near_sources,
    near_blocks,
    far_rows,
    far_sources,
    far_left,
    far_right,
):
    headings, panels = incident.shape
    incident = jnp.pad(incident, ((0, ROWS - headings), (0, 0)))
    near, block = near_blocks.shape[:2]
    far, rank = far_left.shape[:2]
    clusters = panels // block
    slots = clusters + 2 * REACH + CAPACITY * owners
    smem = pl.BlockSpec(memory_space=pltpu.SMEM)
    vmem = pl.BlockSpec(memory_space=pltpu.VMEM)
    meta_size = 3 * (near + far) + 2 * (clusters + 1)
    meta, asks = pl.pallas_call(
        functools.partial(prepare, clusters, owners),
        out_shape=(
            jax.ShapeDtypeStruct((meta_size,), jnp.int32),
            jax.ShapeDtypeStruct((owners, 1, 128), jnp.int32),
        ),
        in_specs=[smem] * 4,
        out_specs=(smem, smem),
        scratch_shapes=[
            pltpu.SMEM((clusters + 1,), jnp.int32),
            pltpu.SMEM((clusters + 1,), jnp.int32),
            pltpu.SMEM((owners,), jnp.int32),
        ],
    )(near_rows, near_sources, far_rows, far_sources)
    bf, f32 = jnp.bfloat16, jnp.float32
    dma = pltpu.SemaphoreType.DMA
    image = jax.ShapeDtypeStruct((ROWS, panels), f32)
    first, second, inverse = pl.pallas_call(
        functools.partial(kernel, clusters, owners, shares, near, far),
        out_shape=(
            image,
            jax.ShapeDtypeStruct((clusters, ROWS, block), f32),
            jax.ShapeDtypeStruct((clusters, block), jnp.int32),
        ),
        in_specs=[vmem, vmem, vmem, smem, pl.BlockSpec(memory_space=pl.ANY), vmem, vmem],
        out_specs=(vmem, vmem, vmem),
        scratch_shapes=[
            pltpu.VMEM((near, block, block), bf),
            pltpu.VMEM((clusters, ROWS, block), f32),
            pltpu.VMEM((clusters, block), jnp.int32),
            pltpu.VMEM((clusters, ROWS, block), bf),
            pltpu.VMEM((clusters, ROWS, block), bf),
            pltpu.VMEM((slots, shares, ROWS, block), bf),
            pltpu.VMEM((slots, shares, ROWS, block), bf),
            pltpu.VMEM((owners, shares, CAPACITY, ROWS, block), bf),
            pltpu.VMEM((owners, shares, CAPACITY, ROWS, block), bf),
            pltpu.VMEM((near + 1, shares, ROWS, block), f32),
            pltpu.VMEM((far + 1, shares, ROWS, block), f32),
            pltpu.VMEM((shares, clusters, ROWS, block), bf),
            pltpu.VMEM((shares, clusters, ROWS, block), bf),
            pltpu.VMEM((shares, clusters, ROWS, block), bf),
            pltpu.VMEM((shares, clusters, ROWS, block), bf),
            pltpu.VMEM((owners, shares, 1, 128), jnp.int32),
            pltpu.SMEM((owners, shares, 1, 128), jnp.int32),
            pltpu.VMEM((ROWS, block), f32),
            pltpu.VMEM((owners, ROWS, block), f32),
            dma,
            dma,
            dma,
            dma,
            dma((2,)),
            dma((2,)),
            dma((2,)),
            dma((2, CHUNKS, shares)),
            dma,
            dma,
        ],
        compiler_params=pltpu.CompilerParams(
            collective_id=0, has_side_effects=True, vmem_limit_bytes=56 * 2**20
        ),
    )(
        incident,
        tree_order.reshape(clusters, block),
        asks,
        meta,
        near_blocks,
        far_left,
        far_right,
    )
    anywhere = pl.BlockSpec(memory_space=pl.ANY)
    first, second = pl.pallas_call(
        functools.partial(finish, clusters),
        out_shape=(image, image),
        in_specs=[vmem, vmem, vmem],
        out_specs=(anywhere, anywhere),
        scratch_shapes=[pltpu.VMEM((ROWS, panels), f32), dma((CHUNKS + 1,))],
        compiler_params=pltpu.CompilerParams(vmem_limit_bytes=16 * 2**20),
    )(first, second, inverse)
    return first[:headings], second[:headings]


def solution(mesh):
    lists = ("groups", "panels", "rhs")
    in_specs = (
        P("rhs", ("groups", "panels")),
        P(("groups", "panels")),
        P(lists),
        P(lists),
        P(lists, None, None),
        P(lists),
        P(lists),
        P(lists, None, None),
        P(lists, None, None),
    )
    out_specs = (P("rhs", ("groups", "panels")), P("rhs", ("groups", "panels")))
    return jax.shard_map(
        functools.partial(on_device, mesh.shape["panels"], mesh.shape["rhs"]),
        mesh=mesh,
        in_specs=in_specs,
        out_specs=out_specs,
        check_vma=False,
    )
```

```python
import functools

import jax
import jax.numpy as jnp
from jax import lax
from jax.experimental import pallas as pl
from jax.experimental.pallas import tpu as pltpu
from jax.sharding import PartitionSpec as P

MESH = pl.DeviceIdType.MESH
REACH = 2
CAPACITY = 2
LAST = (((1,), (1,)), ((), ()))
CHUNKS = 4
ROWS = 16


def sort_list(rows_ref, count, clusters, meta, base, cnt, start, index_of):
    perm, index, keep, end = base, base + count, base + 2 * count, base + 3 * count

    def clear(c, _):
        cnt[c] = 0
        return 0

    lax.fori_loop(0, clusters + 1, clear, 0, unroll=True)

    def tally(e, _):
        r = rows_ref[e]
        cnt[r] = cnt[r] + 1
        return 0

    lax.fori_loop(0, count, tally, 0, unroll=8)

    def prefix(c, run):
        n = cnt[c]
        cnt[c] = run
        start[c] = run
        meta[end + c] = jnp.where(n > 0, run + n - 1, count)
        return run + n

    lax.fori_loop(0, clusters + 1, prefix, 0, unroll=True)

    def place(e, _):
        r = rows_ref[e]
        pos = cnt[r]
        cnt[r] = pos + 1
        meta[perm + pos] = e
        meta[index + pos] = index_of(e)
        meta[keep + pos] = jnp.where(pos == start[r], 0, 1)
        return 0

    lax.fori_loop(0, count, place, 0, unroll=8)
    return end + clusters + 1


def prepare(clusters, owners, near_rows, near_sources, far_rows, far_sources, meta, asks, cnt, start, seen):
    owner = lax.axis_index("panels")
    near, far = near_rows.shape[0], far_rows.shape[0]
    first = owner * clusters - REACH

    def near_index(e):
        return near_sources[e] - first

    base = sort_list(near_rows, near, clusters, meta, 0, cnt, start, near_index)

    def clear(q, _):
        seen[q] = 0
        return 0

    lax.fori_loop(0, owners, clear, 0, unroll=True)

    def far_index(e):
        source = far_sources[e]
        target = source // clusters
        within = source - target * clusters
        slot = seen[target]
        seen[target] = slot + 1
        asks[target, 0, slot] = within
        return jnp.where(
            target == owner, within + REACH, clusters + 2 * REACH + CAPACITY * target + slot
        )

    sort_list(far_rows, far, clusters, meta, base, cnt, start, far_index)


def permute(source, index_ref, clusters, emit):
    for t in range(clusters):
        index = jnp.broadcast_to(index_ref[t : t + 1, :], (ROWS, 128))
        low, high = index & 127, index >> 7
        tile = jnp.zeros((ROWS, 128), jnp.float32)
        for s in range(clusters):
            moved = jnp.take_along_axis(source[s], low, axis=1, mode="promise_in_bounds")
            tile = jnp.where(high == s, moved, tile)
        emit(t, tile)


def kernel(
    clusters,
    owners,
    shares,
    near,
    far,
    incident,
    order,
    asks,
    meta,
    near_hbm,
    far_left,
    far_right,
    first_image,
    second_tree,
    inverse,
    blocks,
    values,
    local,
    own_a,
    own_b,
    table_a,
    table_b,
    stage_a,
    stage_b,
    near_sums,
    far_sums,
    send_a,
    send_b,
    recv_a,
    recv_b,
    asked_v,
    asked_s,
    squares,
    all_squares,
    load_sem,
    asked_sem,
    ask_send,
    ask_recv,
    out_sem,
    in_sem,
    sum_send,
    sum_recv,
    sq_send,
    sq_recv,
):
    p = lax.axis_index("panels")
    r = lax.axis_index("rhs")
    span = clusters // CHUNKS
    slots = clusters + 2 * REACH

    load = pltpu.make_async_copy(near_hbm, blocks, load_sem)
    load.start()

    def peers(body):
        def step(j, _):
            q = lax.rem(p + j, owners)
            for s in range(shares):
                body(q, s)
            return 0

        lax.fori_loop(1, owners, step, 0)

    def others(body):
        for j in range(1, shares):
            body(lax.rem(r + j, shares))

    barrier = pltpu.get_barrier_semaphore()

    def greet(q, s):
        pl.semaphore_signal(
            barrier, inc=1, device_id={"panels": q, "rhs": s}, device_id_type=MESH
        )

    peers(greet)
    others(lambda s: greet(p, s))

    asked_v[p] = jnp.zeros_like(asked_v[p])
    for s in range(clusters):
        values[s] = incident[:, s * 128 : (s + 1) * 128].astype(jnp.float32)
    local[...] = order[...] - p * (clusters * 128)
    near_sums[near] = jnp.zeros_like(near_sums[near])
    far_sums[far] = jnp.zeros_like(far_sums[far])

    pl.semaphore_wait(barrier, shares * owners - 1)

    def ask_copy(q, s, src_owner, src_rhs):
        return pltpu.make_async_remote_copy(
            src_ref=asks.at[q],
            dst_ref=asked_v.at[src_owner, src_rhs],
            send_sem=ask_send,
            recv_sem=ask_recv,
            device_id={"panels": q, "rhs": s},
            device_id_type=MESH,
        )

    peers(lambda q, s: ask_copy(q, s, p, r).start())

    def half_copy(phase, own, table, k, s, src_rhs):
        return pltpu.make_async_remote_copy(
            src_ref=own.at[pl.ds(k * span, span)],
            dst_ref=table.at[pl.ds(REACH + k * span, span), src_rhs],
            send_sem=out_sem.at[phase],
            recv_sem=in_sem.at[phase],
            device_id={"panels": p, "rhs": s},
            device_id_type=MESH,
        )

    def seg_copy(phase, stage, table, q, s, src_owner, src_rhs):
        return pltpu.make_async_remote_copy(
            src_ref=stage.at[q, s],
            dst_ref=table.at[pl.ds(slots + CAPACITY * src_owner, CAPACITY), src_rhs],
            send_sem=out_sem.at[phase],
            recv_sem=in_sem.at[phase],
            device_id={"panels": q, "rhs": s},
            device_id_type=MESH,
        )

    def halo_copy(phase, own, table, up, q, s, src_rhs):
        src, dst = (clusters - REACH, 0) if up else (0, clusters + REACH)
        return pltpu.make_async_remote_copy(
            src_ref=own.at[pl.ds(src, REACH)],
            dst_ref=table.at[pl.ds(dst, REACH), src_rhs],
            send_sem=out_sem.at[phase],
            recv_sem=in_sem.at[phase],
            device_id={"panels": q, "rhs": s},
            device_id_type=MESH,
        )

    def spread(phase, own, table, stage):
        for s in range(shares):
            halo_copy(phase, own, table, True, lax.rem(p + 1, owners), s, r).start()
            halo_copy(phase, own, table, False, lax.rem(p + owners - 1, owners), s, r).start()

        def serve(q, s):
            for k in range(CAPACITY):
                stage[q, s, k] = own[asked_s[q, s, 0, k]]
            seg_copy(phase, stage, table, q, s, p, r).start()

        peers(serve)

    moved = (shares - 1) * clusters // shares + (owners - 1) * CAPACITY + 2 * REACH

    def wait_bytes(view, sem):
        pltpu.make_async_copy(view, view, sem).wait()

    def gathered(phase, table):
        wait_bytes(table.at[pl.ds(0, moved)], in_sem.at[phase])

    base = 3 * near + clusters + 1

    def apply(table):
        def far_step(i, acc):
            segment = table[meta[base + far + i]].reshape(shares * ROWS, 128)
            entry = meta[base + i]
            coefficients = lax.dot_general(
                segment, far_right[entry], LAST, preferred_element_type=jnp.float32
            ).astype(jnp.bfloat16)
            term = jnp.dot(coefficients, far_left[entry], preferred_element_type=jnp.float32)
            acc = acc * meta[base + 2 * far + i].astype(jnp.float32) + term
            far_sums[i] = acc.reshape(shares, ROWS, 128)
            return acc

        rows = shares * ROWS
        group = 2 if near % 2 == 0 else 1

        def near_step(g, acc):
            places = [g * group + k for k in range(group)]
            segments = [table[meta[near + i]].reshape(rows, 128) for i in places]
            weights = [blocks[meta[i]] for i in places]
            terms = lax.dot_general(
                jnp.concatenate(segments, axis=0),
                jnp.concatenate(weights, axis=0),
                LAST,
                preferred_element_type=jnp.float32,
            )
            for k, i in enumerate(places):
                term = terms[k * rows : (k + 1) * rows, k * 128 : (k + 1) * 128]
                acc = acc * meta[2 * near + i].astype(jnp.float32) + term
                near_sums[i] = acc.reshape(shares, ROWS, 128)
            return acc

        zero = jnp.zeros((rows, 128), jnp.float32)
        steps = near // group
        lax.fori_loop(0, far, far_step, zero, unroll=far if shares <= 2 else 2)
        lax.fori_loop(0, steps, near_step, zero, unroll=steps if shares <= 2 else 2)

    def part(c, s):
        return (
            near_sums[meta[3 * near + c], s] + far_sums[meta[base + 3 * far + c], s]
        )

    def sum_copy(phase, send, recv, k, s, src_rhs):
        return pltpu.make_async_remote_copy(
            src_ref=send.at[s, pl.ds(k * span, span)],
            dst_ref=recv.at[src_rhs, pl.ds(k * span, span)],
            send_sem=sum_send.at[phase],
            recv_sem=sum_recv.at[phase, k, src_rhs],
            device_id={"panels": p, "rhs": s},
            device_id_type=MESH,
        )

    def reduce(phase, send, recv, take, after):
        def give(k, s):
            for c in range(k * span, (k + 1) * span):
                send[s, c] = part(c, s).astype(jnp.bfloat16)
            sum_copy(phase, send, recv, k, s, r).start()

        for k in range(CHUNKS):
            others(lambda s: give(k, s))
        for k in range(CHUNKS):
            others(lambda s: sum_copy(phase, send, recv, k, s, s).wait_recv())
            for c in range(k * span, (k + 1) * span):
                tile = part(c, r)
                for j in range(1, shares):
                    tile = tile + recv[lax.rem(r + j, shares), c]
                take(c, tile)
            after(k)

    def tree_tile(t, tile):
        tile = tile.astype(jnp.bfloat16)
        own_a[t] = tile
        table_a[REACH + t, r] = tile

    permute(values, local, clusters, tree_tile)
    for k in range(CHUNKS):
        others(lambda s: half_copy(0, own_a, table_a, k, s, r).start())
    wait_bytes(asked_v.at[pl.ds(0, owners - 1)], ask_recv)
    to_scalar = pltpu.make_async_copy(asked_v, asked_s, asked_sem)
    to_scalar.start()
    to_scalar.wait()
    spread(0, own_a, table_a, stage_a)

    digits = jnp.zeros((2 * clusters, 128), jnp.float32)
    lane = lax.broadcasted_iota(jnp.int32, (1, 128), 1)
    for s in range(clusters):
        row = local[s : s + 1, :]
        groups = lax.broadcasted_iota(jnp.int32, (clusters, 128), 0) == (row >> 7)
        position = lane + s * 128
        top = jnp.where(groups, (position >> 6).astype(jnp.float32), 0.0)
        bottom = jnp.where(groups, (position & 63).astype(jnp.float32), 0.0)
        left = jnp.concatenate([top, bottom], axis=0).astype(jnp.bfloat16)
        hot = lax.broadcasted_iota(jnp.int32, (128, 128), 0) == (row & 127)
        hot = jnp.where(hot, 1.0, 0.0).astype(jnp.bfloat16)
        digits = digits + lax.dot_general(left, hot, LAST, preferred_element_type=jnp.float32)
    inverse[...] = (digits[:clusters] * 64.0 + digits[clusters:]).astype(jnp.int32)

    load.wait()
    gathered(0, table_a)
    apply(table_a)

    squares[...] = jnp.zeros_like(squares)

    def first_tile(c, tile):
        values[c] = tile
        squares[...] += tile * tile
        tile = tile.astype(jnp.bfloat16)
        own_b[c] = tile
        table_b[REACH + c, r] = tile

    def share(k):
        others(lambda s: half_copy(1, own_b, table_b, k, s, r).start())

    reduce(0, send_a, recv_a, first_tile, share)
    spread(1, own_b, table_b, stage_b)

    def sq_copy(q, src_owner):
        return pltpu.make_async_remote_copy(
            src_ref=squares,
            dst_ref=all_squares.at[src_owner],
            send_sem=sq_send,
            recv_sem=sq_recv,
            device_id={"panels": q, "rhs": r},
            device_id_type=MESH,
        )

    def same(body):
        def step(j, _):
            body(lax.rem(p + j, owners))
            return 0

        lax.fori_loop(1, owners, step, 0)

    same(lambda q: sq_copy(q, p).start())
    all_squares[p] = squares[...]

    def first_out(t, tile):
        first_image[:, t * 128 : (t + 1) * 128] = tile

    permute(values, inverse, clusters, first_out)

    gathered(1, table_b)
    apply(table_b)
    wait_bytes(all_squares.at[pl.ds(0, owners - 1)], sq_recv)
    total = lax.fori_loop(
        0, owners, lambda q, acc: acc + all_squares[q], jnp.zeros((ROWS, 128), jnp.float32)
    )
    total = jnp.sum(total, axis=1, keepdims=True)
    scale = lax.rsqrt(total / (clusters * 128 * owners) + 1e-06)

    def second_tile(c, tile):
        second_tree[c] = tile * scale

    reduce(1, send_b, recv_b, second_tile, lambda k: None)

    wait_bytes(asked_v.at[pl.ds(0, owners - 1)], ask_send)
    wait_bytes(table_a.at[pl.ds(0, moved)], out_sem.at[0])
    wait_bytes(table_b.at[pl.ds(0, moved)], out_sem.at[1])
    wait_bytes(send_a.at[pl.ds(0, shares - 1)], sum_send.at[0])
    wait_bytes(send_b.at[pl.ds(0, shares - 1)], sum_send.at[1])
    wait_bytes(all_squares.at[pl.ds(0, owners - 1)], sq_send)


def finish(
    clusters, first_hbm, second_hbm, inverse_hbm, first_image, second_image, first, tree, inverse, tiles, sems
):
    loads = [
        pltpu.make_async_copy(src, dst, sems.at[CHUNKS + k])
        for k, (src, dst) in enumerate(((inverse_hbm, inverse), (second_hbm, tree), (first_hbm, first)))
    ]
    for load in loads:
        load.start()
    span = clusters // CHUNKS
    copies = []

    def emit(t, tile):
        tiles[:, t * 128 : (t + 1) * 128] = tile
        if t % span == span - 1:
            k = t // span
            columns = pl.ds(k * span * 128, span * 128)
            copies.append(
                pltpu.make_async_copy(tiles.at[:, columns], second_image.at[:, columns], sems.at[k])
            )
            copies[-1].start()

    loads[0].wait()
    loads[1].wait()
    permute(tree, inverse, clusters, emit)
    loads[2].wait()
    copies.append(pltpu.make_async_copy(first, first_image, sems.at[CHUNKS + 3]))
    copies[-1].start()
    for copy in copies:
        copy.wait()


def on_device(
    owners,
    shares,
    incident,
    tree_order,
    near_rows,
    near_sources,
    near_blocks,
    far_rows,
    far_sources,
    far_left,
    far_right,
):
    headings, panels = incident.shape
    incident = jnp.pad(incident, ((0, ROWS - headings), (0, 0)))
    near, block = near_blocks.shape[:2]
    far, rank = far_left.shape[:2]
    clusters = panels // block
    slots = clusters + 2 * REACH + CAPACITY * owners
    smem = pl.BlockSpec(memory_space=pltpu.SMEM)
    vmem = pl.BlockSpec(memory_space=pltpu.VMEM)
    meta_size = 3 * (near + far) + 2 * (clusters + 1)
    meta, asks = pl.pallas_call(
        functools.partial(prepare, clusters, owners),
        out_shape=(
            jax.ShapeDtypeStruct((meta_size,), jnp.int32),
            jax.ShapeDtypeStruct((owners, 1, 128), jnp.int32),
        ),
        in_specs=[smem] * 4,
        out_specs=(smem, smem),
        scratch_shapes=[
            pltpu.SMEM((clusters + 1,), jnp.int32),
            pltpu.SMEM((clusters + 1,), jnp.int32),
            pltpu.SMEM((owners,), jnp.int32),
        ],
    )(near_rows, near_sources, far_rows, far_sources)
    bf, f32 = jnp.bfloat16, jnp.float32
    dma = pltpu.SemaphoreType.DMA
    image = jax.ShapeDtypeStruct((ROWS, panels), f32)
    first, second, inverse = pl.pallas_call(
        functools.partial(kernel, clusters, owners, shares, near, far),
        out_shape=(
            image,
            jax.ShapeDtypeStruct((clusters, ROWS, block), f32),
            jax.ShapeDtypeStruct((clusters, block), jnp.int32),
        ),
        in_specs=[vmem, vmem, vmem, smem, pl.BlockSpec(memory_space=pl.ANY), vmem, vmem],
        out_specs=(vmem, vmem, vmem),
        scratch_shapes=[
            pltpu.VMEM((near, block, block), bf),
            pltpu.VMEM((clusters, ROWS, block), f32),
            pltpu.VMEM((clusters, block), jnp.int32),
            pltpu.VMEM((clusters, ROWS, block), bf),
            pltpu.VMEM((clusters, ROWS, block), bf),
            pltpu.VMEM((slots, shares, ROWS, block), bf),
            pltpu.VMEM((slots, shares, ROWS, block), bf),
            pltpu.VMEM((owners, shares, CAPACITY, ROWS, block), bf),
            pltpu.VMEM((owners, shares, CAPACITY, ROWS, block), bf),
            pltpu.VMEM((near + 1, shares, ROWS, block), f32),
            pltpu.VMEM((far + 1, shares, ROWS, block), f32),
            pltpu.VMEM((shares, clusters, ROWS, block), bf),
            pltpu.VMEM((shares, clusters, ROWS, block), bf),
            pltpu.VMEM((shares, clusters, ROWS, block), bf),
            pltpu.VMEM((shares, clusters, ROWS, block), bf),
            pltpu.VMEM((owners, shares, 1, 128), jnp.int32),
            pltpu.SMEM((owners, shares, 1, 128), jnp.int32),
            pltpu.VMEM((ROWS, block), f32),
            pltpu.VMEM((owners, ROWS, block), f32),
            dma,
            dma,
            dma,
            dma,
            dma((2,)),
            dma((2,)),
            dma((2,)),
            dma((2, CHUNKS, shares)),
            dma,
            dma,
        ],
        compiler_params=pltpu.CompilerParams(
            collective_id=0, has_side_effects=True, vmem_limit_bytes=56 * 2**20
        ),
    )(
        incident,
        tree_order.reshape(clusters, block),
        asks,
        meta,
        near_blocks,
        far_left,
        far_right,
    )
    anywhere = pl.BlockSpec(memory_space=pl.ANY)
    first, second = pl.pallas_call(
        functools.partial(finish, clusters),
        out_shape=(image, image),
        in_specs=[anywhere, anywhere, anywhere],
        out_specs=(anywhere, anywhere),
        scratch_shapes=[
            pltpu.VMEM((ROWS, panels), f32),
            pltpu.VMEM((clusters, ROWS, block), f32),
            pltpu.VMEM((clusters, block), jnp.int32),
            pltpu.VMEM((ROWS, panels), f32),
            dma((CHUNKS + 4,)),
        ],
        compiler_params=pltpu.CompilerParams(vmem_limit_bytes=56 * 2**20),
    )(first, second, inverse)
    return first[:headings], second[:headings]


def solution(mesh):
    lists = ("groups", "panels", "rhs")
    in_specs = (
        P("rhs", ("groups", "panels")),
        P(("groups", "panels")),
        P(lists),
        P(lists),
        P(lists, None, None),
        P(lists),
        P(lists),
        P(lists, None, None),
        P(lists, None, None),
    )
    out_specs = (P("rhs", ("groups", "panels")), P("rhs", ("groups", "panels")))
    return jax.shard_map(
        functools.partial(on_device, mesh.shape["panels"], mesh.shape["rhs"]),
        mesh=mesh,
        in_specs=in_specs,
        out_specs=out_specs,
        check_vma=False,
    )
```
